256 devices in a mesh: section: 16 (over z_lo, x), sp: 16 (over y, z_hi, core).
Axes of the slice: x: 4, y: 4, z: 8 (z_hi: 2, z_lo: 4; z = z_hi * 4 + z_lo), core: 2. Of those that a mesh axis runs over, the one named last changes fastest.
Arguments:
- latents: bfloat16 [4, 256, 3072], P(None, 'sp'), may hold values from -6 to 6
- in_flight: bfloat16 [16, 256, 3072], P('section', 'sp'), may hold values from -6 to 6
- modulation: float32 [16, 3, 3072], P('section'), may hold values from -3 to 3
- w_qkv: bfloat16 [16, 3072, 3, 2048], P('section', None, None, 'sp'), may hold values from -0.109375 to 0.109375
- w_expand: bfloat16 [16, 3072, 10240], P('section', None, 'sp'), may hold values from -0.109375 to 0.109375
- qk_gain: float32 [16, 2, 128], P('section'), may hold values from 0.3 to 3
- w_out: bfloat16 [16, 2048, 3072], P('section', 'sp'), may hold values from -0.0546875 to 0.0546875
- w_contract: bfloat16 [16, 10240, 3072], P('section', 'sp'), may hold values from -0.0546875 to 0.0546875
- stale_kv: bfloat16 [16, 2, 1024, 2048], P('section', None, None, 'sp'), may hold values from -400 to 400, as said below
Outputs:
- section_out: bfloat16 [16, 4, 256, 3072], P('section', None, 'sp')
- fresh_kv: bfloat16 [16, 4, 2, 256, 2048], P('section', None, None, None, 'sp')
The draws below stay inside these ranges and needn't reach their ends.
Inputs may be any that keep to these rules, and one draw needn't show every extreme that they name: `stale_kv`: entry 0 holds keys and entry 1 values; patch m occupies rows m * 256 to (m + 1) * 256 - 1.
All inputs are finite; a program needn't handle non-finite values.
Results may differ from the reference program's by a relative error of at most 0.03.
Values may be sent and summed in bfloat16 or wider, within the bound.
A program may use at most 128 MiB of HBM per device.

```python
import math
import jax
import jax.numpy as jnp
from jax import lax

D = 3072
HD = 128
HEADS = 16
FF = 10240
MICRO = 4
SECTIONS = 16
PATCH = 256
CONTEXT = 1024
HEADS_DEV = 1
FF_DEV = 640
N_SP = 16


def draw_stale_kv(key, part):
    key = jax.random.fold_in(key, 7)
    factors = jnp.exp(jax.random.uniform(jax.random.fold_in(key, 1), (SECTIONS, 2, CONTEXT, 1), jnp.float32, math.log(0.3), math.log(2.5)))
    entries = jax.random.normal(jax.random.fold_in(key, 2), (SECTIONS, 2, CONTEXT, HEADS * HD), jnp.float32) * factors
    return entries.astype(jnp.bfloat16)


def levels(key, dims, pieces, smallest, top_value):
    def one(dim, shards_of):
        heights = jax.random.uniform(jax.random.fold_in(jax.random.fold_in(key, 6), dim), (shards_of,), jnp.float32, smallest / len(pieces), top_value / len(pieces))
        return jnp.repeat(jnp.exp(heights), dims[dim] // shards_of).reshape((-1,) + (1,) * (len(dims) - dim - 1))

    level = one(*pieces[0])
    for cut in pieces[1:]:
        level = level * one(*cut)
    return level


def normal_values(stream_key, extent, scale, bound, split=(), kind=jnp.bfloat16):
    array = scale * jax.random.normal(stream_key, extent, jnp.float32)
    if split:
        array = array * levels(stream_key, extent, split, -0.22, 0.18)
    return jnp.clip(array, -bound, bound).astype(kind)


def setup_inputs(seed: int = 0) -> dict:
    keys = jax.random.split(jax.random.key(seed), 10)
    return {
        "latents": normal_values(keys[0], (MICRO, PATCH, D), 1.0, 6.0, ((1, 16),)),
        "in_flight": normal_values(keys[1], (SECTIONS, PATCH, D), 1.0, 6.0, ((0, 16), (1, 16))),
        "modulation": normal_values(keys[2], (SECTIONS, 3, D), 0.5, 3.0, ((0, 16),), jnp.float32),
        "w_qkv": normal_values(keys[3], (SECTIONS, D, 3, HEADS * HD), D ** -0.5, 0.109375, ((0, 16), (3, 16))),
        "w_expand": normal_values(keys[4], (SECTIONS, D, FF), D ** -0.5, 0.109375, ((0, 16), (2, 16))),
        "qk_gain": jnp.clip(jnp.exp(math.log(3.0) - 2.3025851 * jax.random.uniform(keys[5], (SECTIONS, 2, HD), jnp.float32) ** levels(keys[5], (SECTIONS, 2, HD), ((0, 16),), -0.2, 0.2)), 0.3, 3.0),
        "w_out": normal_values(keys[6], (SECTIONS, HEADS * HD, D), (HEADS * HD + FF) ** -0.5, 0.0546875, ((0, 16), (1, 16))),
        "w_contract": normal_values(keys[7], (SECTIONS, FF, D), (HEADS * HD + FF) ** -0.5, 0.0546875, ((0, 16), (1, 16))),
        "stale_kv": draw_stale_kv(jax.random.fold_in(keys[9], 71), 0),
    }


def modulate(inputs, shift_row, scale_row):
    values = inputs.astype(jnp.float32)
    average = lax.optimization_barrier(jnp.mean(values, axis=-1, keepdims=True))
    centred = values - average
    variance = lax.optimization_barrier(jnp.mean(centred * centred, axis=-1, keepdims=True))
    normed = centred * lax.rsqrt(variance + 1e-06)
    return (normed * (1.0 + scale_row) + shift_row).astype(jnp.bfloat16)

def head_norm(values, gain_row):
    mean_square = lax.optimization_barrier(jnp.mean(values * values, axis=-1, keepdims=True))
    return (values * lax.rsqrt(mean_square + 1e-06) * gain_row).astype(jnp.bfloat16)

def single_block(inputs, modulation, w_qkv, w_expand, qk_gain, w_out, w_contract, stale_pair, patch_number):
    modulated = modulate(inputs, modulation[0], modulation[1])
    flat_weight = w_qkv.reshape(D, 3 * HEADS * HD)
    projected = jnp.dot(modulated, flat_weight, preferred_element_type=jnp.float32).reshape(PATCH, 3, HEADS, HD)
    expanded = jnp.dot(modulated, w_expand, preferred_element_type=jnp.float32)
    activated = jax.nn.gelu(expanded, approximate=True).astype(jnp.bfloat16)
    queries = head_norm(projected[:, 0], qk_gain[0])
    key_rows = head_norm(projected[:, 1], qk_gain[1])
    value_rows = projected[:, 2].astype(jnp.bfloat16)
    fresh_pair = jnp.stack([key_rows.reshape(PATCH, HEADS * HD), value_rows.reshape(PATCH, HEADS * HD)], axis=0)
    first_row = patch_number * PATCH
    merged = stale_pair.at[:, first_row:first_row + PATCH].set(fresh_pair)
    all_keys = merged[0].reshape(CONTEXT, HEADS, HD)
    all_values = merged[1].reshape(CONTEXT, HEADS, HD)
    scores = jnp.einsum('qhd,khd->hqk', queries.astype(jnp.float32), all_keys.astype(jnp.float32)) * HD ** (-0.5)
    highest = lax.optimization_barrier(jnp.max(scores, axis=-1, keepdims=True))
    weights = jnp.exp(scores - highest)
    totals = lax.optimization_barrier(jnp.sum(weights, axis=-1, keepdims=True))
    shares = (weights / totals).astype(jnp.bfloat16)
    mixed_rows = jnp.einsum('hqk,khd->qhd', shares.astype(jnp.float32), all_values.astype(jnp.float32)).astype(jnp.bfloat16)
    grouped = jnp.concatenate([mixed_rows.reshape(PATCH, N_SP, HEADS_DEV * HD), activated.reshape(PATCH, N_SP, FF_DEV)], axis=2)
    grouped_weight = jnp.concatenate([w_out.reshape(N_SP, HEADS_DEV * HD, D), w_contract.reshape(N_SP, FF_DEV, D)], axis=1)
    partials = jnp.einsum('pgc,gcd->gpd', grouped.astype(jnp.float32), grouped_weight.astype(jnp.float32)).astype(jnp.bfloat16)
    head_sum = lax.optimization_barrier(jnp.sum(partials.astype(jnp.float32), axis=0))
    result = (inputs.astype(jnp.float32) + modulation[2] * head_sum).astype(jnp.bfloat16)
    return (result, fresh_pair)

def reference(latents, in_flight, modulation, w_qkv, w_expand, qk_gain, w_out, w_contract, stale_kv):
    outputs = [[None] * MICRO for section_number in range(SECTIONS)]
    fresh_all = [[None] * MICRO for section_number in range(SECTIONS)]
    for tick_number in range(MICRO):
        for section_number in range(SECTIONS):
            if section_number == 0:
                inputs = latents[tick_number]
            elif tick_number == 0:
                inputs = in_flight[section_number]
            else:
                inputs = outputs[section_number - 1][tick_number - 1]
            patch_number = (tick_number - section_number) % MICRO
            result, fresh_pair = single_block(inputs, modulation[section_number], w_qkv[section_number], w_expand[section_number], qk_gain[section_number], w_out[section_number], w_contract[section_number], stale_kv[section_number], patch_number)
            outputs[section_number][tick_number] = result
            fresh_all[section_number][patch_number] = fresh_pair
    section_out = jnp.stack([jnp.stack(row_list, axis=0) for row_list in outputs], axis=0)
    fresh_kv = jnp.stack([jnp.stack(row_list, axis=0) for row_list in fresh_all], axis=0)
    return (section_out, fresh_kv)
```

```python
import jax
import jax.numpy as jnp
from jax import lax
from jax.experimental import pallas as pl
from jax.experimental.pallas import tpu as pltpu
from jax.sharding import PartitionSpec as P

MESH = pl.DeviceIdType.MESH
F32 = jnp.float32
BF16 = jnp.bfloat16
D = 3072
HD = 128
FFD = 640
ROWS = 16
PATCH = 256
CONTEXT = 1024
MICRO = 4
NSEC = 16
NC = 2
CW = D // NC
HALF = 128


def modulate(u, shift_row, scale_row):
    average = jnp.mean(u, axis=-1, keepdims=True)
    centred = u - average
    variance = jnp.mean(centred * centred, axis=-1, keepdims=True)
    normed = centred * lax.rsqrt(variance + 1e-06)
    return (normed * (1.0 + scale_row) + shift_row).astype(BF16)


def head_norm(values, gain_row):
    mean_square = jnp.mean(values * values, axis=-1, keepdims=True)
    return (values * lax.rsqrt(mean_square + 1e-06) * gain_row).astype(BF16)


def kernel(
    lat_ref, infl_ref, mod_ref, wqkv_ref, wexp_ref, gain_ref, wout_ref, wcon_ref, stale_ref,
    sec_ref, fresh_ref,
    win, wo, stale, kvw, lat, u_own, u_cur, mods, cat, q_buf, part, rx_d, r_buf, rx_y, t_buf, rx_x, ret_src, ret_rx,
    load_sem, iu_s, iu_r, lat_s, lat_r, ag_ys, ag_yr, ag_cs, ag_cr, rd_s, rd_r, ry_s, ry_r, x_s, x_r, ret_s, ret_r,
):
    s = lax.axis_index("section")
    p = lax.axis_index("sp")
    y = p // 4
    zh = lax.rem(p // 2, 2)
    c = lax.rem(p, 2)
    oc = 1 - c
    oz = 1 - zh
    s_next = lax.rem(s + 1, NSEC)
    s_prev = lax.rem(s + NSEC - 1, NSEC)

    def dev(section, yy, zz, cc):
        return {"section": section, "sp": (yy * 2 + zz) * 2 + cc}

    sibling = dev(s, y, zh, oc)
    zpart = dev(s, y, oz, c)
    ypeer = {d: dev(s, lax.rem(y + d, 4), zh, c) for d in (1, 2, 3)}
    nxt = (dev(s_next, y, zh, c), dev(s_next, y, oz, c))
    prv = (dev(s_prev, y, zh, c), dev(s_prev, y, oz, c))

    loads = [
        pltpu.make_async_copy(wqkv_ref, win.at[:, pl.ds(0, 3 * HD)], load_sem.at[0]),
        pltpu.make_async_copy(wexp_ref.at[0], win.at[:, pl.ds(3 * HD, FFD)], load_sem.at[1]),
        pltpu.make_async_copy(wout_ref.at[0], wo.at[pl.ds(0, HD)], load_sem.at[2]),
        pltpu.make_async_copy(wcon_ref.at[0], wo.at[pl.ds(HD, FFD)], load_sem.at[3]),
        pltpu.make_async_copy(stale_ref.at[0], stale, load_sem.at[4]),
    ]
    for load in loads:
        load.start()

    barrier = pltpu.get_barrier_semaphore()
    friends = [sibling, zpart, ypeer[1], ypeer[2], ypeer[3], nxt[0], nxt[1], prv[0], prv[1]]
    for friend in friends:
        pl.semaphore_signal(barrier, inc=1, device_id=friend, device_id_type=MESH)
    pl.semaphore_wait(barrier, len(friends))

    def remote(src, dst, ssem, rsem, target):
        return pltpu.make_async_remote_copy(
            src_ref=src, dst_ref=dst, send_sem=ssem, recv_sem=rsem, device_id=target, device_id_type=MESH
        )

    def c_init():
        return remote(u_own, u_cur.at[zh], iu_s, iu_r, zpart)

    def c_lat():
        return remote(lat.at[0], lat.at[1], lat_s, lat_r, zpart)

    def c_ag_y(j, z, d):
        slot = mods.at[j, z, c, y]
        return remote(slot, slot, ag_ys.at[j, z, d], ag_yr.at[j, z, d], ypeer[d])

    def c_ag_c(j, z, d):
        slot = mods.at[j, z, c, lax.rem(y + 4 - d, 4)]
        return remote(slot, slot, ag_cs.at[j, z, d], ag_cr.at[j, z, d], sibling)

    def cols(h):
        return pl.ds(h * CW, CW)

    def c_rd(j, z, h):
        return remote(
            part.at[z, oc, :, :, cols(h)], rx_d.at[j, z, :, :, cols(h)], rd_s.at[j, z, h], rd_r.at[j, z, h], sibling
        )

    def c_ry(j, z, h, d):
        return remote(
            r_buf.at[j, z, d, :, cols(h)], rx_y.at[j, z, d, :, cols(h)], ry_s.at[j, z, h, d], ry_r.at[j, z, h, d], ypeer[d]
        )

    def c_x(j, z, h, k):
        return remote(
            t_buf.at[j, z, :, cols(h)], rx_x.at[j, z, k, :, cols(h)], x_s.at[j, z, h, k], x_r.at[j, z, h, k], nxt[k]
        )

    def c_last(h):
        return remote(
            t_buf.at[MICRO - 1, oz, :, cols(h)], rx_x.at[MICRO - 1, 0, 1, :, cols(h)],
            x_s.at[MICRO - 1, 0, h, 1], x_r.at[MICRO - 1, 0, h, 1], zpart,
        )

    def c_ret(j):
        return remote(ret_src.at[j], ret_rx.at[j], ret_s.at[j], ret_r.at[j], prv[0])

    def norm_and_gather(j, z, u):
        mods[j, z, c, y] = modulate(u, mod_ref[0, 0:1], mod_ref[0, 1:2])
        for d in (2, 1, 3):
            c_ag_y(j, z, d).start()
        c_ag_c(j, z, 0).start()

    lat[0] = lat_ref[...]
    u_own[...] = jnp.where(s == 0, lat_ref[0], infl_ref[0])
    c_init().start()

    @pl.when(s == 0)
    def _():
        c_lat().start()

    u_cur[zh] = u_own[...]
    c_init().wait_recv()
    for z in range(2):
        norm_and_gather(0, z, u_cur[z].astype(F32))

    @pl.when(s == 0)
    def _():
        c_lat().wait_recv()

    for load in loads:
        load.wait()

    def body(j, carry):
        m = lax.rem(j - s + 2 * NSEC, MICRO)
        kvw[...] = stale[...]

        def gathered(z):
            for d in (1, 3, 2):
                c_ag_y(j, z, d).wait_recv()
                c_ag_c(j, z, d).start()
            for d in (0, 1, 3, 2):
                c_ag_c(j, z, d).wait_recv()

        def project(z):
            rows = mods[j, z].reshape(HALF, D)
            first = jnp.dot(rows, win[:, 0:512], preferred_element_type=F32)
            q_buf[z] = head_norm(first[:, 0:128], gain_ref[0, 0:1])
            keys = head_norm(first[:, 128:256], gain_ref[0, 1:2])
            values = first[:, 256:384].astype(BF16)
            for cc in range(2):
                for yy in range(4):
                    local_row = (cc * 4 + yy) * ROWS
                    row = yy * 64 + z * 32 + cc * 16
                    for k, new in ((0, keys), (1, values)):
                        block = new[local_row:local_row + ROWS]
                        kvw[k, pl.ds(pl.multiple_of(m * PATCH + row, ROWS), ROWS)] = block
                        fresh_ref[0, m, k, row:row + ROWS] = block
            cat[z, :, 128:256] = jax.nn.gelu(first[:, 384:512], approximate=True).astype(BF16)

        def expand(z):
            rows = mods[j, z].reshape(HALF, D)
            second = jnp.dot(rows, win[:, 512:1024], preferred_element_type=F32)
            cat[z, :, 256:768] = jax.nn.gelu(second, approximate=True).astype(BF16)

        def attend(z):
            scores = lax.dot_general(
                q_buf[z], kvw[0], (((1,), (1,)), ((), ())), preferred_element_type=F32
            ) * HD ** (-0.5)
            highest = jnp.max(scores, axis=-1, keepdims=True)
            weights = jnp.exp(scores - highest)
            totals = jnp.sum(weights, axis=-1, keepdims=True)
            shares = (weights / totals).astype(BF16)
            cat[z, :, 0:128] = jnp.dot(shares, kvw[1], preferred_element_type=F32).astype(BF16)

        def contract(z, h):
            product = jnp.dot(cat[z], wo[:, h * CW:(h + 1) * CW], preferred_element_type=F32)
            part[z, :, :, :, h * CW:(h + 1) * CW] = product.astype(BF16).reshape(2, 4, ROWS, CW)
            c_rd(j, z, h).start()

        def pair_sum(z, h):
            lo = h * CW
            c_rd(j, z, h).wait_recv()
            for d in (2, 1, 3):
                yy = lax.rem(y + d, 4)
                total = part[z, c, yy, :, lo:lo + CW].astype(F32) + rx_d[j, z, yy, :, lo:lo + CW].astype(F32)
                r_buf[j, z, d, :, lo:lo + CW] = total.astype(BF16)
                c_ry(j, z, h, d).start()

        def y_sum(z, h):
            lo = h * CW
            total = part[z, c, y, :, lo:lo + CW].astype(F32) + rx_d[j, z, y, :, lo:lo + CW].astype(F32)
            for d in (1, 3, 2):
                c_ry(j, z, h, d).wait_recv()
            for d in (1, 3, 2):
                total = total + rx_y[j, z, d, :, lo:lo + CW].astype(F32)
            total = total * mod_ref[0, 2:3, lo:lo + CW]
            base = u_cur[z, :, lo:lo + CW].astype(F32)
            total = total + jnp.where(zh == z, base, 0.0)
            t_buf[j, z, :, lo:lo + CW] = total.astype(BF16)

            @pl.when(j < MICRO - 1)
            def _():
                c_x(j, z, h, 1).start()
                c_x(j, z, h, 0).start()

        gathered(0)
        project(0)
        expand(0)
        gathered(1)
        project(1)
        attend(0)
        for h in range(NC):
            contract(0, h)
        expand(1)
        attend(1)
        for h in range(NC):
            pair_sum(0, h)
        for h in range(NC):
            contract(1, h)
        for h in range(NC):
            pair_sum(1, h)
        for z in range(2):
            for h in range(NC):
                y_sum(z, h)

        for z in range(2):
            for h in range(NC):
                c_rd(j, z, h).wait_send()

        @pl.when(j < MICRO - 1)
        def _():
            for z in range(2):
                for h in range(NC):
                    for k in range(2):
                        c_x(j, z, h, k).wait_recv()
                summed = (rx_x[j, z, 0].astype(F32) + rx_x[j, z, 1].astype(F32)).astype(BF16)

                @pl.when(zh == z)
                def _():
                    ret_src[j] = summed
                    c_ret(j).start()

                u_new = jnp.where(s == 0, jnp.where(zh == z, lat[0, j + 1], lat[1, j + 1]), summed)
                u_cur[z] = u_new
                norm_and_gather(j + 1, z, u_new.astype(F32))

        return carry

    lax.fori_loop(0, MICRO, body, 0)

    for h in range(NC):
        c_last(h).start()
    for h in range(NC):
        c_last(h).wait_recv()
    final = t_buf[MICRO - 1, zh].astype(F32) + rx_x[MICRO - 1, 0, 1].astype(F32)
    sec_ref[0, MICRO - 1] = final.astype(BF16)

    def finish(j, carry):
        c_ret(j).wait_recv()
        sec_ref[0, j] = ret_rx[j]
        c_ret(j).wait_send()
        for z in range(2):
            for h in range(NC):
                for k in range(2):
                    c_x(j, z, h, k).wait_send()
        return carry

    lax.fori_loop(0, MICRO - 1, finish, 0)

    def drain(j, carry):
        for z in range(2):
            for d in (1, 2, 3):
                c_ag_y(j, z, d).wait_send()
            for d in range(4):
                c_ag_c(j, z, d).wait_send()
            for h in range(NC):
                for d in (1, 2, 3):
                    c_ry(j, z, h, d).wait_send()
        return carry

    lax.fori_loop(0, MICRO, drain, 0)
    for h in range(NC):
        c_last(h).wait_send()
    c_init().wait_send()

    @pl.when(s == 0)
    def _():
        c_lat().wait_send()


def local(latents, in_flight, modulation, w_qkv, w_expand, qk_gain, w_out, w_contract, stale_kv):
    w_qkv = w_qkv[0].reshape(D, 3 * HD)
    vmem = pl.BlockSpec(memory_space=pltpu.VMEM)
    hbm = pl.BlockSpec(memory_space=pl.ANY)
    dma = pltpu.SemaphoreType.DMA
    return pl.pallas_call(
        kernel,
        out_shape=(
            jax.ShapeDtypeStruct((1, MICRO, ROWS, D), BF16),
            jax.ShapeDtypeStruct((1, MICRO, 2, PATCH, HD), BF16),
        ),
        in_specs=[vmem, vmem, vmem, hbm, hbm, vmem, hbm, hbm, hbm],
        out_specs=(vmem, vmem),
        scratch_shapes=[
            pltpu.VMEM((D, 3 * HD + FFD), BF16),
            pltpu.VMEM((HD + FFD, D), BF16),
            pltpu.VMEM((2, CONTEXT, HD), BF16),
            pltpu.VMEM((2, CONTEXT, HD), BF16),
            pltpu.VMEM((2, MICRO, ROWS, D), BF16),
            pltpu.VMEM((ROWS, D), BF16),
            pltpu.VMEM((2, ROWS, D), BF16),
            pltpu.VMEM((MICRO, 2, 2, 4, ROWS, D), BF16),
            pltpu.VMEM((2, HALF, HD + FFD), BF16),
            pltpu.VMEM((2, HALF, HD), BF16),
            pltpu.VMEM((2, 2, 4, ROWS, D), BF16),
            pltpu.VMEM((MICRO, 2, 4, ROWS, D), BF16),
            pltpu.VMEM((MICRO, 2, 4, ROWS, D), BF16),
            pltpu.VMEM((MICRO, 2, 4, ROWS, D), BF16),
            pltpu.VMEM((MICRO, 2, ROWS, D), BF16),
            pltpu.VMEM((MICRO, 2, 2, ROWS, D), BF16),
            pltpu.VMEM((MICRO - 1, ROWS, D), BF16),
            pltpu.VMEM((MICRO - 1, ROWS, D), BF16),
            dma((5,)),
            dma, dma, dma, dma,
            dma((MICRO, 2, 4)), dma((MICRO, 2, 4)),
            dma((MICRO, 2, 4)), dma((MICRO, 2, 4)),
            dma((MICRO, 2, NC)), dma((MICRO, 2, NC)),
            dma((MICRO, 2, NC, 4)), dma((MICRO, 2, NC, 4)),
            dma((MICRO, 2, NC, 2)), dma((MICRO, 2, NC, 2)),
            dma((MICRO - 1,)), dma((MICRO - 1,)),
        ],
        compiler_params=pltpu.CompilerParams(
            collective_id=0, has_side_effects=True, vmem_limit_bytes=60 * 2**20
        ),
        name="blocks",
    )(latents, in_flight, modulation, w_qkv, w_expand, qk_gain, w_out, w_contract, stale_kv)


def solution(mesh):
    placed = (
        P(None, "sp", None),
        P("section", "sp", None),
        P("section", None, None),
        P("section", None, None, "sp"),
        P("section", None, "sp"),
        P("section", None, None),
        P("section", "sp", None),
        P("section", "sp", None),
        P("section", None, None, "sp"),
    )
    return jax.shard_map(
        local,
        mesh=mesh,
        in_specs=placed,
        out_specs=(P("section", None, "sp", None), P("section", None, None, None, "sp")),
        check_vma=False,
    )
```

```python
import jax
import jax.numpy as jnp
from jax import lax
from jax.experimental import pallas as pl
from jax.experimental.pallas import tpu as pltpu
from jax.sharding import PartitionSpec as P

MESH = pl.DeviceIdType.MESH
F32 = jnp.float32
BF16 = jnp.bfloat16
D = 3072
HD = 128
FFD = 640
ROWS = 16
PATCH = 256
CONTEXT = 1024
MICRO = 4
NSEC = 16
NC = 2
CW = D // NC
GW = D // 2
HALF = 128


def modulate(u, shift_row, scale_row):
    average = jnp.mean(u, axis=-1, keepdims=True)
    centred = u - average
    variance = jnp.mean(centred * centred, axis=-1, keepdims=True)
    normed = centred * lax.rsqrt(variance + 1e-06)
    return (normed * (1.0 + scale_row) + shift_row).astype(BF16)


def head_norm(values, gain_row):
    mean_square = jnp.mean(values * values, axis=-1, keepdims=True)
    return (values * lax.rsqrt(mean_square + 1e-06) * gain_row).astype(BF16)


def kernel(
    lat_ref, infl_ref, mod_ref, wqkv_ref, wexp_ref, gain_ref, wout_ref, wcon_ref, stale_ref,
    sec_ref, fresh_ref,
    win, wo, stale, kvw, lat, u_own, mods, cat, hidden, q_buf, part, rx_d, r_buf, rx_y, t_buf, rx_x, ret_src, sec_buf, fresh_buf,
    load_sem, iu_s, iu_r, lat_s, lat_r, ag_ys, ag_yr, ag_cs, ag_cr, rd_s, rd_r, ry_s, ry_r, x_s, x_r, ret_s, ret_r, sec_sem, fresh_sem,
):
    s = lax.axis_index("section")
    p = lax.axis_index("sp")
    y = p // 4
    zh = lax.rem(p // 2, 2)
    c = lax.rem(p, 2)
    oc = 1 - c
    oz = 1 - zh
    s_next = lax.rem(s + 1, NSEC)
    s_prev = lax.rem(s + NSEC - 1, NSEC)

    def dev(section, yy, zz, cc):
        return {"section": section, "sp": (yy * 2 + zz) * 2 + cc}

    sibling = dev(s, y, zh, oc)
    zpart = dev(s, y, oz, c)
    up = dev(s, lax.rem(y + 1, 4), zh, c)
    down = dev(s, lax.rem(y + 3, 4), zh, c)
    far = dev(s, lax.rem(y + 2, 4), zh, c)
    nxt = (dev(s_next, y, zh, c), dev(s_next, y, oz, c))
    prv = (dev(s_prev, y, zh, c), dev(s_prev, y, oz, c))

    loads = [
        pltpu.make_async_copy(wqkv_ref.at[1], win.at[:, pl.ds(0, HD)], load_sem.at[0]),
        pltpu.make_async_copy(wqkv_ref.at[2], win.at[:, pl.ds(HD, HD)], load_sem.at[1]),
        pltpu.make_async_copy(wqkv_ref.at[0], win.at[:, pl.ds(2 * HD, HD)], load_sem.at[2]),
        pltpu.make_async_copy(wexp_ref.at[0], win.at[:, pl.ds(3 * HD, FFD)], load_sem.at[3]),
        pltpu.make_async_copy(wout_ref.at[0], wo.at[pl.ds(0, HD)], load_sem.at[4]),
        pltpu.make_async_copy(wcon_ref.at[0], wo.at[pl.ds(HD, FFD)], load_sem.at[5]),
        pltpu.make_async_copy(stale_ref.at[0], stale, load_sem.at[6]),
    ]
    for load in loads:
        load.start()

    barrier = pltpu.get_barrier_semaphore()
    friends = [sibling, zpart, up, down, far, nxt[0], nxt[1], prv[0], prv[1]]
    for friend in friends:
        pl.semaphore_signal(barrier, inc=1, device_id=friend, device_id_type=MESH)
    pl.semaphore_wait(barrier, len(friends))

    def remote(src, dst, ssem, rsem, target):
        return pltpu.make_async_remote_copy(
            src_ref=src, dst_ref=dst, send_sem=ssem, recv_sem=rsem, device_id=target, device_id_type=MESH
        )

    def c_init(g):
        half = mods.at[0, c, zh, y, :, pl.ds(g * GW, GW)]
        return remote(half, half, iu_s.at[g], iu_r.at[g], zpart)

    def c_lat():
        return remote(lat.at[0, pl.ds(1, MICRO - 1)], lat.at[1, pl.ds(1, MICRO - 1)], lat_s, lat_r, zpart)

    def c_ag_y(j, z, kind):
        half = mods.at[j, c, z, y, :, pl.ds((kind % 2) * GW, GW)]
        return remote(half, half, ag_ys.at[j, z, kind], ag_yr.at[j, z, kind], (far, up, down)[kind // 2])

    def c_ag_c(j, z, d):
        slot = mods.at[j, c, z, lax.rem(y + 4 - d, 4)]
        return remote(slot, slot, ag_cs.at[j, z, d], ag_cr.at[j, z, d], sibling)

    def cols(h):
        return pl.ds(h * CW, CW)

    def c_rd(j, z, h):
        return remote(
            part.at[oc, z, :, :, cols(h)], rx_d.at[j, z, :, :, cols(h)], rd_s.at[j, z, h], rd_r.at[j, z, h], sibling
        )

    def c_ry(j, z, h, d):
        return remote(
            r_buf.at[j, z, d, :, cols(h)], rx_y.at[j, z, d, :, cols(h)],
            ry_s.at[j, z, h, d], ry_r.at[j, z, h, d], {1: up, 2: far, 3: down}[d],
        )

    def c_x(j, z, h, k):
        return remote(
            t_buf.at[j, z, :, cols(h)], rx_x.at[j, z, k, :, cols(h)], x_s.at[j, z, h, k], x_r.at[j, z, h, k], nxt[k]
        )

    def c_last(h):
        return remote(
            t_buf.at[MICRO - 1, oz, :, cols(h)], rx_x.at[MICRO - 1, 0, 1, :, cols(h)],
            x_s.at[MICRO - 1, 0, h, 1], x_r.at[MICRO - 1, 0, h, 1], zpart,
        )

    def c_ret(j):
        return remote(ret_src.at[j], sec_buf.at[j], ret_s.at[j], ret_r.at[j], prv[0])

    def norm(j, z, u):
        mods[j, c, z, y] = modulate(u, mod_ref[0], mod_ref[1])

    def gather(j, z):
        for kind in range(6):
            c_ag_y(j, z, kind).start()
        c_ag_c(j, z, 0).start()

    lat[0] = lat_ref[...]
    u_own[...] = jnp.where(s == 0, lat_ref[0], infl_ref[0])
    norm(0, zh, u_own[...].astype(F32))
    for g in range(2):
        c_init(g).start()
    gather(0, zh)
    for g in range(2):
        c_init(g).wait_recv()
        for kind in (0, 2, 4):
            c_ag_y(0, oz, kind + g).start()
    c_ag_c(0, oz, 0).start()

    @pl.when(s == 0)
    def _():
        c_lat().start()

    for load in loads:
        load.wait()

    def body(j, carry):
        m = lax.rem(j - s + 2 * NSEC, MICRO)
        kvw[...] = stale[...]

        def forward(z):
            for d in (1, 3, 2):
                for g in range(2):
                    c_ag_y(j, z, {2: 0, 1: 2, 3: 4}[d] + g).wait_recv()
                c_ag_c(j, z, d).start()

        def gathered(k):
            @pl.when(c == k)
            def _():
                for z in range(2):
                    forward(z)

            @pl.when(c != k)
            def _():
                for z in range(2):
                    for d in (0, 1, 3, 2):
                        c_ag_c(j, z, d).wait_recv()

        def keys_values(k):
            rows = mods[j, k].reshape(HALF, D)
            pair = jnp.dot(rows, win[:, 0:256], preferred_element_type=F32)
            keys = head_norm(pair[:, 0:128], gain_ref[0, 1:2])
            values = pair[:, 128:256].astype(BF16)
            for z in range(2):
                for yy in range(4):
                    local_row = (z * 4 + yy) * ROWS
                    row = yy * 64 + z * 32 + k * 16
                    for i, new in ((0, keys), (1, values)):
                        block = new[local_row:local_row + ROWS]
                        kvw[i, pl.ds(pl.multiple_of(m * PATCH + row, ROWS), ROWS)] = block
                        fresh_buf[m, i, row:row + ROWS] = block

        def queries(k):
            rows = mods[j, k].reshape(HALF, D)
            pair = jnp.dot(rows, win[:, 256:512], preferred_element_type=F32)
            q_buf[k] = head_norm(pair[:, 0:128], gain_ref[0, 0:1])
            cat[k, :, 128:256] = jax.nn.gelu(pair[:, 128:256], approximate=True).astype(BF16)

        def expand(k):
            rows = mods[j, k].reshape(HALF, D)
            second = jnp.dot(rows, win[:, 512:1024], preferred_element_type=F32)
            cat[k, :, 256:768] = jax.nn.gelu(second, approximate=True).astype(BF16)

        def attend(k):
            scores = lax.dot_general(
                q_buf[k], kvw[0], (((1,), (1,)), ((), ())), preferred_element_type=F32
            ) * HD ** (-0.5)
            highest = jnp.max(scores, axis=-1, keepdims=True)
            weights = jnp.exp(scores - highest)
            totals = jnp.sum(weights, axis=-1, keepdims=True)
            shares = (weights / totals).astype(BF16)
            cat[k, :, 0:128] = jnp.dot(shares, kvw[1], preferred_element_type=F32).astype(BF16)

        def hidden_part():
            for h in range(NC):
                columns = slice(h * CW, (h + 1) * CW)
                hidden[:, columns] = jnp.dot(cat[0, :, HD:], wo[HD:, columns], preferred_element_type=F32)

        def contract(k, h):
            columns = slice(h * CW, (h + 1) * CW)

            def whole():
                product = jnp.dot(cat[k], wo[:, columns], preferred_element_type=F32)
                part[k, :, :, :, columns] = product.astype(BF16).reshape(2, 4, ROWS, CW)

            def rest():
                product = hidden[:, columns] + jnp.dot(
                    cat[k, :, 0:HD], wo[0:HD, columns], preferred_element_type=F32
                )
                part[k, :, :, :, columns] = product.astype(BF16).reshape(2, 4, ROWS, CW)

            if k == 0:
                pl.when(c == 0)(rest)
                pl.when(c == 1)(whole)
            else:
                whole()

            @pl.when(c != k)
            def _():
                for z in range(2):
                    c_rd(j, z, h).start()

        def pair_sum(z, h):
            lo = h * CW
            c_rd(j, z, h).wait_recv()
            for d in (2, 1, 3):
                yy = lax.rem(y + d, 4)
                r_buf[j, z, d, :, lo:lo + CW] = part[c, z, yy, :, lo:lo + CW] + rx_d[j, z, yy, :, lo:lo + CW]
                c_ry(j, z, h, d).start()

        def y_sum(z, h):
            lo = h * CW
            total = part[c, z, y, :, lo:lo + CW].astype(F32) + rx_d[j, z, y, :, lo:lo + CW].astype(F32)
            for d in (1, 3, 2):
                c_ry(j, z, h, d).wait_recv()
            for d in (1, 3, 2):
                total = total + rx_y[j, z, d, :, lo:lo + CW].astype(F32)
            total = total * mod_ref[2, :, lo:lo + CW]
            base = u_own[:, lo:lo + CW].astype(F32)
            total = total + jnp.where(zh == z, base, 0.0)
            t_buf[j, z, :, lo:lo + CW] = total.astype(BF16)

            @pl.when(j < MICRO - 1)
            def _():
                c_x(j, z, h, 1).start()
                c_x(j, z, h, 0).start()

            @pl.when(jnp.logical_and(j == MICRO - 1, oz == z))
            def _():
                c_last(h).start()

        def on_core(k, *steps):
            @pl.when(c == k)
            def _():
                for step, z, h in steps:
                    step(z, h)

        def on_core(k, *steps):
            @pl.when(c == k)
            def _():
                for step, z, h in steps:
                    step(z, h)

        gathered(0)
        @pl.when(c == 1)
        def _():
            forward(0)

        keys_values(0)
        queries(0)
        @pl.when(c == 1)
        def _():
            forward(1)

        expand(0)
        @pl.when(c == 0)
        def _():
            hidden_part()
            for z in range(2):
                for d in (0, 1, 3, 2):
                    c_ag_c(j, z, d).wait_recv()

        keys_values(1)
        attend(0)
        contract(0, 0)
        contract(0, 1)
        on_core(0, (pair_sum, 0, 0))
        queries(1)
        on_core(0, (pair_sum, 0, 1))
        expand(1)
        on_core(0, (pair_sum, 1, 0), (pair_sum, 1, 1))
        attend(1)
        contract(1, 0)
        on_core(0, (y_sum, 0, 0))
        contract(1, 1)
        on_core(0, (y_sum, 0, 1), (y_sum, 1, 0), (y_sum, 1, 1))
        on_core(1, (pair_sum, 0, 0), (pair_sum, 0, 1), (pair_sum, 1, 0), (pair_sum, 1, 1))
        on_core(1, (y_sum, 0, 0), (y_sum, 0, 1), (y_sum, 1, 0), (y_sum, 1, 1))

        def fresh_out():
            return pltpu.make_async_copy(fresh_buf.at[m], fresh_ref.at[0, m], fresh_sem.at[m])

        fresh_out().start()

        for z in range(2):
            for h in range(NC):
                c_rd(j, z, h).wait_send()

        @pl.when(jnp.logical_and(s == 0, j == 0))
        def _():
            c_lat().wait_recv()

        @pl.when(j < MICRO - 1)
        def _():
            for z in range(2):
                for h in range(NC):
                    for k in range(2):
                        c_x(j, z, h, k).wait_recv()
                summed = (rx_x[j, z, 0].astype(F32) + rx_x[j, z, 1].astype(F32)).astype(BF16)

                @pl.when(zh == z)
                def _():
                    ret_src[j] = summed
                    c_ret(j).start()

                u_new = jnp.where(s == 0, jnp.where(zh == z, lat[0, j + 1], lat[1, j + 1]), summed)

                @pl.when(zh == z)
                def _():
                    u_own[...] = u_new

                norm(j + 1, z, u_new.astype(F32))
                gather(j + 1, z)

        return carry

    lax.fori_loop(0, MICRO, body, 0)

    def sec_out(j):
        return pltpu.make_async_copy(sec_buf.at[j], sec_ref.at[0, j], sec_sem.at[j])

    for h in range(NC):
        lo = h * CW
        c_last(h).wait_recv()
        final = t_buf[MICRO - 1, zh, :, lo:lo + CW].astype(F32) + rx_x[MICRO - 1, 0, 1, :, lo:lo + CW].astype(F32)
        sec_buf[MICRO - 1, :, lo:lo + CW] = final.astype(BF16)
    sec_out(MICRO - 1).start()

    def finish(j, carry):
        c_ret(j).wait_recv()
        sec_out(j).start()
        c_ret(j).wait_send()
        for z in range(2):
            for h in range(NC):
                for k in range(2):
                    c_x(j, z, h, k).wait_send()
        return carry

    lax.fori_loop(0, MICRO - 1, finish, 0)

    def drain(j, carry):
        for z in range(2):
            for kind in range(6):
                c_ag_y(j, z, kind).wait_send()
            for d in range(4):
                c_ag_c(j, z, d).wait_send()
            for h in range(NC):
                for d in (1, 2, 3):
                    c_ry(j, z, h, d).wait_send()
        return carry

    lax.fori_loop(0, MICRO, drain, 0)
    for h in range(NC):
        c_last(h).wait_send()
    for j in range(MICRO):
        sec_out(j).wait()
        pltpu.make_async_copy(fresh_buf.at[j], fresh_ref.at[0, j], fresh_sem.at[j]).wait()
    for g in range(2):
        c_init(g).wait_send()

    @pl.when(s == 0)
    def _():
        c_lat().wait_send()


def place(sec_in, fresh_in, sec_out, fresh_out, sec_buf, fresh_buf, in_sem, out_sem):
    pairs = ((sec_in, sec_buf, sec_out), (fresh_in, fresh_buf, fresh_out))

    def arrive(k, j):
        return pltpu.make_async_copy(pairs[k][0].at[0, j], pairs[k][1].at[j], in_sem.at[k, j])

    def leave(k, j):
        return pltpu.make_async_copy(pairs[k][1].at[j], pairs[k][2].at[0, j], out_sem.at[k, j])

    steps = [(k, j) for j in range(MICRO) for k in range(2)]
    for step in steps:
        arrive(*step).start()
    for step in steps:
        arrive(*step).wait()
        leave(*step).start()
    for step in steps:
        leave(*step).wait()


def local(latents, in_flight, modulation, w_qkv, w_expand, qk_gain, w_out, w_contract, stale_kv):
    w_qkv = jnp.transpose(w_qkv[0], (1, 0, 2))
    modulation = jnp.transpose(modulation, (1, 0, 2))
    vmem = pl.BlockSpec(memory_space=pltpu.VMEM)
    hbm = pl.BlockSpec(memory_space=pl.ANY)
    dma = pltpu.SemaphoreType.DMA
    parts = pl.pallas_call(
        kernel,
        out_shape=(
            jax.ShapeDtypeStruct((1, MICRO, ROWS, D), BF16),
            jax.ShapeDtypeStruct((1, MICRO, 2, PATCH, HD), BF16),
        ),
        in_specs=[vmem, vmem, vmem, hbm, hbm, vmem, hbm, hbm, hbm],
        out_specs=(hbm, hbm),
        scratch_shapes=[
            pltpu.VMEM((D, 3 * HD + FFD), BF16),
            pltpu.VMEM((HD + FFD, D), BF16),
            pltpu.VMEM((2, CONTEXT, HD), BF16),
            pltpu.VMEM((2, CONTEXT, HD), BF16),
            pltpu.VMEM((2, MICRO, ROWS, D), BF16),
            pltpu.VMEM((ROWS, D), BF16),
            pltpu.VMEM((MICRO, 2, 2, 4, ROWS, D), BF16),
            pltpu.VMEM((2, HALF, HD + FFD), BF16),
            pltpu.VMEM((HALF, D), F32),
            pltpu.VMEM((2, HALF, HD), BF16),
            pltpu.VMEM((2, 2, 4, ROWS, D), BF16),
            pltpu.VMEM((MICRO, 2, 4, ROWS, D), BF16),
            pltpu.VMEM((MICRO, 2, 4, ROWS, D), BF16),
            pltpu.VMEM((MICRO, 2, 4, ROWS, D), BF16),
            pltpu.VMEM((MICRO, 2, ROWS, D), BF16),
            pltpu.VMEM((MICRO, 2, 2, ROWS, D), BF16),
            pltpu.VMEM((MICRO - 1, ROWS, D), BF16),
            pltpu.VMEM((MICRO, ROWS, D), BF16),
            pltpu.VMEM((MICRO, 2, PATCH, HD), BF16),
            dma((7,)),
            dma((2,)), dma((2,)), dma, dma,
            dma((MICRO, 2, 6)), dma((MICRO, 2, 6)),
            dma((MICRO, 2, 4)), dma((MICRO, 2, 4)),
            dma((MICRO, 2, NC)), dma((MICRO, 2, NC)),
            dma((MICRO, 2, NC, 4)), dma((MICRO, 2, NC, 4)),
            dma((MICRO, 2, NC, 2)), dma((MICRO, 2, NC, 2)),
            dma((MICRO - 1,)), dma((MICRO - 1,)),
            dma((MICRO,)), dma((MICRO,)),
        ],
        compiler_params=pltpu.CompilerParams(
            collective_id=0, has_side_effects=True, vmem_limit_bytes=60 * 2**20
        ),
        name="blocks",
    )(latents, in_flight, modulation, w_qkv, w_expand, qk_gain, w_out, w_contract, stale_kv)
    return pl.pallas_call(
        place,
        out_shape=tuple(jax.ShapeDtypeStruct(part.shape, part.dtype) for part in parts),
        in_specs=[hbm, hbm],
        out_specs=(hbm, hbm),
        scratch_shapes=[
            pltpu.VMEM((MICRO, ROWS, D), BF16),
            pltpu.VMEM((MICRO, 2, PATCH, HD), BF16),
            dma((2, MICRO)),
            dma((2, MICRO)),
        ],
        name="place",
    )(*parts)


def solution(mesh):
    placed = (
        P(None, "sp", None),
        P("section", "sp", None),
        P("section", None, None),
        P("section", None, None, "sp"),
        P("section", None, "sp"),
        P("section", None, None),
        P("section", "sp", None),
        P("section", "sp", None),
        P("section", None, None, "sp"),
    )
    return jax.shard_map(
        local,
        mesh=mesh,
        in_specs=placed,
        out_specs=(P("section", None, "sp", None), P("section", None, None, None, "sp")),
        check_vma=False,
    )
```

```python
import jax
import jax.numpy as jnp
from jax import lax
from jax.experimental import pallas as pl
from jax.experimental.pallas import tpu as pltpu
from jax.sharding import PartitionSpec as P

MESH = pl.DeviceIdType.MESH
F32 = jnp.float32
BF16 = jnp.bfloat16
D = 3072
HD = 128
FFD = 640
ROWS = 16
PATCH = 256
CONTEXT = 1024
MICRO = 4
NSEC = 16
NC = 2
CW = D // NC
GW = D // 2
HALF = 128
LOG2E = 1.4426950408889634


def modulate(u, shift_row, scale_row):
    average = jnp.mean(u, axis=-1, keepdims=True)
    centred = u - average
    variance = jnp.mean(centred * centred, axis=-1, keepdims=True)
    normed = centred * lax.rsqrt(variance + 1e-06)
    return (normed * (1.0 + scale_row) + shift_row).astype(BF16)


def head_norm(values, gain_row):
    mean_square = jnp.mean(values * values, axis=-1, keepdims=True)
    return (values * lax.rsqrt(mean_square + 1e-06) * gain_row).astype(BF16)


def kernel(
    lat_ref, infl_ref, mod_ref, wqkv_ref, wexp_ref, gain_ref, wout_ref, wcon_ref, stale_ref,
    sec_ref, fresh_ref,
    win, wo, stale, kvw, lat, u_own, mods, cat, hidden, q_buf, part, rx_d, r_buf, rx_y, t_buf, rx_x, ret_src, sec_buf, fresh_buf,
    load_sem, iu_s, iu_r, lat_s, lat_r, ag_ys, ag_yr, ag_cs, ag_cr, rd_s, rd_r, ry_s, ry_r, x_s, x_r, ret_s, ret_r, sec_sem, fresh_sem,
):
    s = lax.axis_index("section")
    p = lax.axis_index("sp")
    y = p // 4
    zh = lax.rem(p // 2, 2)
    c = lax.rem(p, 2)
    oc = 1 - c
    oz = 1 - zh
    s_next = lax.rem(s + 1, NSEC)
    s_prev = lax.rem(s + NSEC - 1, NSEC)

    def dev(section, yy, zz, cc):
        return {"section": section, "sp": (yy * 2 + zz) * 2 + cc}

    sibling = dev(s, y, zh, oc)
    zpart = dev(s, y, oz, c)
    up = dev(s, lax.rem(y + 1, 4), zh, c)
    down = dev(s, lax.rem(y + 3, 4), zh, c)
    far = dev(s, lax.rem(y + 2, 4), zh, c)
    nxt = (dev(s_next, y, zh, c), dev(s_next, y, oz, c))
    prv = (dev(s_prev, y, zh, c), dev(s_prev, y, oz, c))

    loads = [
        pltpu.make_async_copy(wqkv_ref.at[1], win.at[:, pl.ds(0, HD)], load_sem.at[0]),
        pltpu.make_async_copy(wqkv_ref.at[2], win.at[:, pl.ds(HD, HD)], load_sem.at[1]),
        pltpu.make_async_copy(wqkv_ref.at[0], win.at[:, pl.ds(2 * HD, HD)], load_sem.at[2]),
        pltpu.make_async_copy(wexp_ref.at[0], win.at[:, pl.ds(3 * HD, FFD)], load_sem.at[3]),
        pltpu.make_async_copy(wout_ref.at[0], wo.at[pl.ds(0, HD)], load_sem.at[4]),
        pltpu.make_async_copy(wcon_ref.at[0], wo.at[pl.ds(HD, FFD)], load_sem.at[5]),
        pltpu.make_async_copy(stale_ref.at[0], stale, load_sem.at[6]),
    ]
    for load in loads:
        load.start()

    barrier = pltpu.get_barrier_semaphore()
    friends = [sibling, zpart, up, down, far, nxt[0], nxt[1], prv[0], prv[1]]
    for friend in friends:
        pl.semaphore_signal(barrier, inc=1, device_id=friend, device_id_type=MESH)

    def remote(src, dst, ssem, rsem, target):
        return pltpu.make_async_remote_copy(
            src_ref=src, dst_ref=dst, send_sem=ssem, recv_sem=rsem, device_id=target, device_id_type=MESH
        )

    def c_init(g):
        half = mods.at[0, c, zh, y, :, pl.ds(g * GW, GW)]
        return remote(half, half, iu_s.at[g], iu_r.at[g], zpart)

    def c_lat():
        return remote(lat.at[0, pl.ds(1, MICRO - 1)], lat.at[1, pl.ds(1, MICRO - 1)], lat_s, lat_r, zpart)

    def c_ag_y(j, z, kind):
        half = mods.at[j, c, z, y, :, pl.ds((kind % 2) * GW, GW)]
        return remote(half, half, ag_ys.at[j, z, kind], ag_yr.at[j, z, kind], (far, up, down)[kind // 2])

    def c_ag_c(j, z, d):
        slot = mods.at[j, c, z, lax.rem(y + 4 - d, 4)]
        return remote(slot, slot, ag_cs.at[j, z, d], ag_cr.at[j, z, d], sibling)

    def cols(h):
        return pl.ds(h * CW, CW)

    def c_rd(j, z, h):
        return remote(
            part.at[oc, z, :, :, cols(h)], rx_d.at[j, z, :, :, cols(h)], rd_s.at[j, z, h], rd_r.at[j, z, h], sibling
        )

    def c_ry(j, z, h, d):
        return remote(
            r_buf.at[j, z, d, :, cols(h)], rx_y.at[j, z, d, :, cols(h)],
            ry_s.at[j, z, h, d], ry_r.at[j, z, h, d], {1: up, 2: far, 3: down}[d],
        )

    def c_x(j, z, h, k):
        return remote(
            t_buf.at[j, z, :, cols(h)], rx_x.at[j, z, k, :, cols(h)], x_s.at[j, z, h, k], x_r.at[j, z, h, k], nxt[k]
        )

    def c_last(h):
        return remote(
            t_buf.at[MICRO - 1, oz, :, cols(h)], rx_x.at[MICRO - 1, 0, 1, :, cols(h)],
            x_s.at[MICRO - 1, 0, h, 1], x_r.at[MICRO - 1, 0, h, 1], zpart,
        )

    def c_ret(j):
        return remote(ret_src.at[j], sec_buf.at[j], ret_s.at[j], ret_r.at[j], prv[0])

    def norm(j, z, u):
        mods[j, c, z, y] = modulate(u, mod_ref[0], mod_ref[1])

    def gather(j, z):
        for kind in range(6):
            c_ag_y(j, z, kind).start()
        c_ag_c(j, z, 0).start()

    lat[0] = lat_ref[...]
    u_own[...] = jnp.where(s == 0, lat_ref[0], infl_ref[0])
    norm(0, zh, u_own[...].astype(F32))
    pl.semaphore_wait(barrier, len(friends))
    for g in range(2):
        c_init(g).start()
    gather(0, zh)
    for g in range(2):
        c_init(g).wait_recv()
        for kind in (0, 2, 4):
            c_ag_y(0, oz, kind + g).start()
    c_ag_c(0, oz, 0).start()

    @pl.when(s == 0)
    def _():
        c_lat().start()

    for load in loads:
        load.wait()

    def body(j, carry):
        m = lax.rem(j - s + 2 * NSEC, MICRO)
        kvw[...] = stale[...]
        last = j // (MICRO - 1)

        def ordered(z):
            return (1 - last) * z + last * lax.rem(oz + z, 2)

        def forward(z):
            for d in (1, 3, 2):
                for g in range(2):
                    c_ag_y(j, z, {2: 0, 1: 2, 3: 4}[d] + g).wait_recv()
                c_ag_c(j, z, d).start()

        def gathered(k):
            @pl.when(c == k)
            def _():
                for z in range(2):
                    forward(z)

            @pl.when(c != k)
            def _():
                for z in range(2):
                    for d in (0, 1, 3, 2):
                        c_ag_c(j, z, d).wait_recv()

        def keys_values(k):
            rows = mods[j, k].reshape(HALF, D)
            pair = jnp.dot(rows, win[:, 0:256], preferred_element_type=F32)
            keys = head_norm(pair[:, 0:128], gain_ref[0, 1:2])
            values = pair[:, 128:256].astype(BF16)
            for z in range(2):
                for yy in range(4):
                    local_row = (z * 4 + yy) * ROWS
                    row = yy * 64 + z * 32 + k * 16
                    for i, new in ((0, keys), (1, values)):
                        block = new[local_row:local_row + ROWS]
                        kvw[i, pl.ds(pl.multiple_of(m * PATCH + row, ROWS), ROWS)] = block
                        fresh_buf[m, i, row:row + ROWS] = block

        def queries(k):
            rows = mods[j, k].reshape(HALF, D)
            pair = jnp.dot(rows, win[:, 256:512], preferred_element_type=F32)
            q_buf[k] = head_norm(pair[:, 0:128], gain_ref[0, 0:1])
            cat[k, :, 128:256] = jax.nn.gelu(pair[:, 128:256], approximate=True).astype(BF16)

        def expand(k):
            rows = mods[j, k].reshape(HALF, D)
            second = jnp.dot(rows, win[:, 512:1024], preferred_element_type=F32)
            cat[k, :, 256:768] = jax.nn.gelu(second, approximate=True).astype(BF16)

        def attend(k):
            scores = lax.dot_general(
                q_buf[k], kvw[0], (((1,), (1,)), ((), ())), preferred_element_type=F32
            )
            highest = jnp.max(scores, axis=-1, keepdims=True)
            weights = jnp.exp2((scores - highest) * (HD ** (-0.5) * LOG2E))
            totals = jnp.sum(weights, axis=-1, keepdims=True)
            shares = (weights * (1.0 / totals)).astype(BF16)
            cat[k, :, 0:128] = jnp.dot(shares, kvw[1], preferred_element_type=F32).astype(BF16)

        def hidden_part():
            for h in range(NC):
                columns = slice(h * CW, (h + 1) * CW)
                hidden[:, columns] = jnp.dot(cat[0, :, HD:], wo[HD:, columns], preferred_element_type=F32)

        def contract(k, h):
            columns = slice(h * CW, (h + 1) * CW)

            def whole():
                product = jnp.dot(cat[k], wo[:, columns], preferred_element_type=F32)
                part[k, :, :, :, columns] = product.astype(BF16).reshape(2, 4, ROWS, CW)

            def rest():
                product = hidden[:, columns] + jnp.dot(
                    cat[k, :, 0:HD], wo[0:HD, columns], preferred_element_type=F32
                )
                part[k, :, :, :, columns] = product.astype(BF16).reshape(2, 4, ROWS, CW)

            if k == 0:
                pl.when(c == 0)(rest)
                pl.when(c == 1)(whole)
            else:
                whole()

            @pl.when(c != k)
            def _():
                for z in range(2):
                    c_rd(j, ordered(z), h).start()

        def pair_sum(z, h):
            lo = h * CW
            c_rd(j, z, h).wait_recv()
            for d in (2, 1, 3):
                yy = lax.rem(y + d, 4)
                r_buf[j, z, d, :, lo:lo + CW] = part[c, z, yy, :, lo:lo + CW] + rx_d[j, z, yy, :, lo:lo + CW]
                c_ry(j, z, h, d).start()

        def y_sum(z, h):
            lo = h * CW
            total = part[c, z, y, :, lo:lo + CW].astype(F32) + rx_d[j, z, y, :, lo:lo + CW].astype(F32)
            for d in (1, 3, 2):
                c_ry(j, z, h, d).wait_recv()
            for d in (1, 3, 2):
                total = total + rx_y[j, z, d, :, lo:lo + CW].astype(F32)
            total = total * mod_ref[2, :, lo:lo + CW]
            base = u_own[:, lo:lo + CW].astype(F32)
            total = total + jnp.where(zh == z, base, 0.0)
            t_buf[j, z, :, lo:lo + CW] = total.astype(BF16)

            @pl.when(j < MICRO - 1)
            def _():
                c_x(j, z, h, 0).start()
                c_x(j, z, h, 1).start()

            @pl.when(jnp.logical_and(j == MICRO - 1, oz == z))
            def _():
                c_last(h).start()

        def on_core(k, *steps):
            @pl.when(c == k)
            def _():
                for step, z, h in steps:
                    step(ordered(z), h)

        gathered(0)
        @pl.when(c == 1)
        def _():
            forward(0)

        keys_values(0)
        queries(0)
        @pl.when(c == 1)
        def _():
            forward(1)

        expand(0)
        @pl.when(c == 0)
        def _():
            hidden_part()
            for z in range(2):
                for d in (0, 1, 3, 2):
                    c_ag_c(j, z, d).wait_recv()

        keys_values(1)
        attend(0)
        contract(0, 0)
        contract(0, 1)
        on_core(0, (pair_sum, 0, 0))
        queries(1)
        on_core(0, (pair_sum, 0, 1))
        expand(1)
        on_core(0, (pair_sum, 1, 0), (pair_sum, 1, 1))
        attend(1)
        on_core(0, (y_sum, 0, 0))
        contract(1, 0)
        on_core(0, (y_sum, 0, 1))
        contract(1, 1)
        on_core(0, (y_sum, 1, 0), (y_sum, 1, 1))
        on_core(1, (pair_sum, 0, 0), (pair_sum, 0, 1), (pair_sum, 1, 0), (pair_sum, 1, 1))
        on_core(1, (y_sum, 0, 0), (y_sum, 0, 1), (y_sum, 1, 0), (y_sum, 1, 1))

        def fresh_out():
            return pltpu.make_async_copy(fresh_buf.at[m], fresh_ref.at[0, m], fresh_sem.at[m])

        fresh_out().start()

        for z in range(2):
            for h in range(NC):
                c_rd(j, z, h).wait_send()

        @pl.when(jnp.logical_and(s == 0, j == 0))
        def _():
            c_lat().wait_recv()

        @pl.when(j < MICRO - 1)
        def _():
            for z in range(2):
                for h in range(NC):
                    for k in range(2):
                        c_x(j, z, h, k).wait_recv()
                summed = (rx_x[j, z, 0].astype(F32) + rx_x[j, z, 1].astype(F32)).astype(BF16)

                u_new = jnp.where(s == 0, jnp.where(zh == z, lat[0, j + 1], lat[1, j + 1]), summed)

                norm(j + 1, z, u_new.astype(F32))
                gather(j + 1, z)

                @pl.when(zh == z)
                def _():
                    u_own[...] = u_new
                    ret_src[j] = summed
                    c_ret(j).start()

        return carry

    lax.fori_loop(0, MICRO, body, 0)

    def sec_out(j):
        return pltpu.make_async_copy(sec_buf.at[j], sec_ref.at[0, j], sec_sem.at[j])

    for h in range(NC):
        lo = h * CW
        c_last(h).wait_recv()
        final = t_buf[MICRO - 1, zh, :, lo:lo + CW].astype(F32) + rx_x[MICRO - 1, 0, 1, :, lo:lo + CW].astype(F32)
        sec_buf[MICRO - 1, :, lo:lo + CW] = final.astype(BF16)
    sec_out(MICRO - 1).start()

    def finish(j, carry):
        c_ret(j).wait_recv()
        sec_out(j).start()
        c_ret(j).wait_send()
        for z in range(2):
            for h in range(NC):
                for k in range(2):
                    c_x(j, z, h, k).wait_send()
        return carry

    lax.fori_loop(0, MICRO - 1, finish, 0)

    def drain(j, carry):
        for z in range(2):
            for kind in range(6):
                c_ag_y(j, z, kind).wait_send()
            for d in range(4):
                c_ag_c(j, z, d).wait_send()
            for h in range(NC):
                for d in (1, 2, 3):
                    c_ry(j, z, h, d).wait_send()
        return carry

    lax.fori_loop(0, MICRO, drain, 0)
    for h in range(NC):
        c_last(h).wait_send()
    for j in range(MICRO):
        sec_out(j).wait()
        pltpu.make_async_copy(fresh_buf.at[j], fresh_ref.at[0, j], fresh_sem.at[j]).wait()
    for g in range(2):
        c_init(g).wait_send()

    @pl.when(s == 0)
    def _():
        c_lat().wait_send()


def place(sec_in, fresh_in, sec_out, fresh_out, sec_buf, fresh_buf, in_sem, out_sem):
    pairs = ((sec_in, sec_buf, sec_out), (fresh_in, fresh_buf, fresh_out))

    def arrive(k, j):
        return pltpu.make_async_copy(pairs[k][0].at[0, j], pairs[k][1].at[j], in_sem.at[k, j])

    def leave(k, j):
        return pltpu.make_async_copy(pairs[k][1].at[j], pairs[k][2].at[0, j], out_sem.at[k, j])

    steps = [(k, j) for j in range(MICRO) for k in range(2)]
    for step in steps:
        arrive(*step).start()
    for step in steps:
        arrive(*step).wait()
        leave(*step).start()
    for step in steps:
        leave(*step).wait()


def local(latents, in_flight, modulation, w_qkv, w_expand, qk_gain, w_out, w_contract, stale_kv):
    w_qkv = jnp.transpose(w_qkv[0], (1, 0, 2))
    modulation = jnp.transpose(modulation, (1, 0, 2))
    vmem = pl.BlockSpec(memory_space=pltpu.VMEM)
    hbm = pl.BlockSpec(memory_space=pl.ANY)
    dma = pltpu.SemaphoreType.DMA
    parts = pl.pallas_call(
        kernel,
        out_shape=(
            jax.ShapeDtypeStruct((1, MICRO, ROWS, D), BF16),
            jax.ShapeDtypeStruct((1, MICRO, 2, PATCH, HD), BF16),
        ),
        in_specs=[vmem, vmem, vmem, hbm, hbm, vmem, hbm, hbm, hbm],
        out_specs=(hbm, hbm),
        scratch_shapes=[
            pltpu.VMEM((D, 3 * HD + FFD), BF16),
            pltpu.VMEM((HD + FFD, D), BF16),
            pltpu.VMEM((2, CONTEXT, HD), BF16),
            pltpu.VMEM((2, CONTEXT, HD), BF16),
            pltpu.VMEM((2, MICRO, ROWS, D), BF16),
            pltpu.VMEM((ROWS, D), BF16),
            pltpu.VMEM((MICRO, 2, 2, 4, ROWS, D), BF16),
            pltpu.VMEM((2, HALF, HD + FFD), BF16),
            pltpu.VMEM((HALF, D), F32),
            pltpu.VMEM((2, HALF, HD), BF16),
            pltpu.VMEM((2, 2, 4, ROWS, D), BF16),
            pltpu.VMEM((MICRO, 2, 4, ROWS, D), BF16),
            pltpu.VMEM((MICRO, 2, 4, ROWS, D), BF16),
            pltpu.VMEM((MICRO, 2, 4, ROWS, D), BF16),
            pltpu.VMEM((MICRO, 2, ROWS, D), BF16),
            pltpu.VMEM((MICRO, 2, 2, ROWS, D), BF16),
            pltpu.VMEM((MICRO - 1, ROWS, D), BF16),
            pltpu.VMEM((MICRO, ROWS, D), BF16),
            pltpu.VMEM((MICRO, 2, PATCH, HD), BF16),
            dma((7,)),
            dma((2,)), dma((2,)), dma, dma,
            dma((MICRO, 2, 6)), dma((MICRO, 2, 6)),
            dma((MICRO, 2, 4)), dma((MICRO, 2, 4)),
            dma((MICRO, 2, NC)), dma((MICRO, 2, NC)),
            dma((MICRO, 2, NC, 4)), dma((MICRO, 2, NC, 4)),
            dma((MICRO, 2, NC, 2)), dma((MICRO, 2, NC, 2)),
            dma((MICRO - 1,)), dma((MICRO - 1,)),
            dma((MICRO,)), dma((MICRO,)),
        ],
        compiler_params=pltpu.CompilerParams(
            collective_id=0, has_side_effects=True, vmem_limit_bytes=60 * 2**20
        ),
        name="blocks",
    )(latents, in_flight, modulation, w_qkv, w_expand, qk_gain, w_out, w_contract, stale_kv)
    return pl.pallas_call(
        place,
        out_shape=tuple(jax.ShapeDtypeStruct(part.shape, part.dtype) for part in parts),
        in_specs=[hbm, hbm],
        out_specs=(hbm, hbm),
        scratch_shapes=[
            pltpu.VMEM((MICRO, ROWS, D), BF16),
            pltpu.VMEM((MICRO, 2, PATCH, HD), BF16),
            dma((2, MICRO)),
            dma((2, MICRO)),
        ],
        name="place",
    )(*parts)


def solution(mesh):
    placed = (
        P(None, "sp", None),
        P("section", "sp", None),
        P("section", None, None),
        P("section", None, None, "sp"),
        P("section", None, "sp"),
        P("section", None, None),
        P("section", "sp", None),
        P("section", "sp", None),
        P("section", None, None, "sp"),
    )
    return jax.shard_map(
        local,
        mesh=mesh,
        in_specs=placed,
        out_specs=(P("section", None, "sp", None), P("section", None, None, None, "sp")),
        check_vma=False,
    )
```
